512 devices in a mesh: dp: 128 (over y, z, core), seq: 4 (over x).
Axes of the slice: x: 4, y: 8, z: 8, core: 2. Of those that a mesh axis runs over, the one named last changes fastest.
Arguments:
- queries: bfloat16 [128, 512, 2048], P('dp', None, 'seq'), may hold values from -20 to 20
- key_states: bfloat16 [128, 512, 2048], P('dp', None, 'seq'), may hold values from -20 to 20
- value_states: bfloat16 [128, 512, 2048], P('dp', None, 'seq'), may hold values from -6 to 6
- grad_out: bfloat16 [128, 512, 4096], P('dp', 'seq'), may hold values from -6 to 6
- out_weight: bfloat16 [4096, 2048], P('dp', 'seq'), may hold values from -0.125 to 0.125
- depths: int32 [128, 512], P('dp'), may hold values from 1 to 4, as said below
- documents: int32 [128, 512], P('dp'), may hold values from 0 to 3, never falling along the last dimension, each value on 1 to 256 neighbouring positions
Outputs:
- grad_queries: bfloat16 [128, 512, 2048], P('dp', None, 'seq')
- grad_keys: bfloat16 [128, 512, 2048], P('dp', None, 'seq')
- grad_values: bfloat16 [128, 512, 2048], P('dp', None, 'seq')
The draws below stay inside these ranges and needn't reach their ends.
Inputs may be any that keep to these rules, and one draw needn't show every extreme that they name: `depths`: in every block of 128 positions of a sequence (the positions of one index of seq) at most 64 tokens have depth 4; in every sequence some block has exactly 64.
All inputs are finite; a program needn't handle non-finite values.
Results may differ from the reference program's by a relative error of at most 0.017.
Values may be sent and summed in bfloat16 or wider, within the bound.
No kernel may reach another device: no remote copies, remote signals or barrier semaphores. Data moves between devices by JAX's collectives and lax.ppermute only.
A program may use at most 64 MiB of HBM per device.

```python
import math
import jax
import jax.numpy as jnp
import numpy as np
from jax import lax

D = 4096
HD = 128
RECUR = 4
GROUP = 128
HW = 2048
ACT_CAP = 64
SEQLEN = 512
SEQS = 128


def draw_queries(key, part):
    key = jax.random.fold_in(key, 2)
    base = jnp.clip(jax.random.normal(key, (SEQS, SEQLEN, HW), jnp.float32), -4.0, 4.0)
    return base.astype(jnp.bfloat16)


def draw_key_states(key, part):
    key = jax.random.fold_in(key, 3)
    base = jnp.clip(jax.random.normal(key, (SEQS, SEQLEN, HW), jnp.float32), -4.0, 4.0)
    return base.astype(jnp.bfloat16)


def draw_depths(key, part):
    key = jax.random.fold_in(key, 1)
    count_key, full_key, order_key, low_key = jax.random.split(key, 4)
    blocks = SEQLEN // GROUP
    counts = jax.random.randint(count_key, (SEQS, blocks), ACT_CAP // 3, ACT_CAP + 1)
    full_block = jax.random.randint(full_key, (SEQS, 1), 0, blocks)
    counts = jnp.where(jnp.arange(blocks)[None, :] == full_block, ACT_CAP, counts)
    noise = jax.random.randint(order_key, (SEQS, blocks, GROUP), 0, 1 << 20) * GROUP + jnp.arange(GROUP, dtype=jnp.int32)
    ranking = jnp.argsort(jnp.argsort(noise, axis=-1), axis=-1)
    active = ranking < counts[:, :, None]
    shallow = jax.random.randint(low_key, (SEQS, blocks, GROUP), 1, RECUR)
    return jnp.where(active, RECUR, shallow).reshape(SEQS, SEQLEN).astype(jnp.int32)


def levels(own_key, extent, pieces, least, top_value):
    gain = 1.0
    for dim, shards_of in pieces:
        draws = jax.random.uniform(jax.random.fold_in(jax.random.fold_in(own_key, 6), dim), (shards_of,), jnp.float32, least / len(pieces), top_value / len(pieces))
        gain = gain * jnp.repeat(jnp.exp(draws), extent[dim] // shards_of).reshape((-1,) + (1,) * (len(extent) - 1 - dim))
    return gain


def length_profile(amount, total, bound, lean):
    portions = [(1 << 20) // math.isqrt(grade ** lean) + 1 for grade in range(2, amount + 1)]
    rest, given = total - bound - (amount - 1), [1] * (amount - 1)
    while rest > 0:
        movable = [i for i in range(amount - 1) if given[i] < bound]
        mass, left = sum([portions[i] for i in movable]), rest
        for i in movable:
            addition = min(bound - given[i], max(1, left * portions[i] // mass), rest)
            given[i] = given[i] + addition
            rest = rest - addition
    return np.array([bound] + given)


def uneven(own_key, number_of, total, limit, slope):
    if number_of == 2:
        one = jax.random.randint(own_key, (), max(1, total - limit), min(limit, total - 1) + 1)
        return jnp.stack([one, total - one])
    tallies = jnp.asarray(length_profile(number_of, total, limit, slope), jnp.int32)
    twos = (number_of - 1) // 2
    donor, taker = tallies[1:1 + 2 * twos:2], tallies[2:2 + 2 * twos:2]
    slack = jnp.minimum(donor - 1, limit - taker)
    moved = jax.random.randint(jax.random.fold_in(own_key, 1), (twos,), 0, 1 << 20) % (slack + 1)
    tallies = tallies.at[1:1 + 2 * twos:2].set(donor - moved).at[2:2 + 2 * twos:2].set(taker + moved)
    return tallies[jax.random.permutation(jax.random.fold_in(own_key, 2), number_of)]


def centred(own_key, dims, scale, bound, shards=(), kind=jnp.bfloat16):
    loudness = levels(own_key, dims, shards, -0.22, 0.18) if shards else 1.0
    entries = jax.random.normal(own_key, dims, jnp.float32) * scale * loudness
    return jnp.minimum(jnp.maximum(entries, -bound), bound).astype(kind)


def setup_inputs(seed: int = 0) -> dict:
    splits = jax.random.split(jax.random.key(seed), 8)
    queries = draw_queries(jax.random.fold_in(splits[7], 71), 0)
    key_states = draw_key_states(jax.random.fold_in(splits[7], 71), 0)
    value_states = centred(splits[2], (SEQS, SEQLEN, HW), 1.0, 6.0, ((0, 128), (2, 4)))
    grad_out = centred(splits[3], (SEQS, SEQLEN, D), 1.0, 6.0, ((0, 128), (1, 4)))
    out_weight = centred(splits[4], (D, HW), HW ** -0.5, 0.125, ((0, 128), (1, 4)))
    depths = draw_depths(jax.random.fold_in(splits[7], 71), 0)
    documents = jax.vmap(lambda own: jnp.searchsorted(jnp.cumsum(uneven(own, 4, SEQLEN, SEQLEN // 2, 1)), jnp.arange(SEQLEN), side="right"))(jax.random.split(splits[6], SEQS)).reshape((SEQS, SEQLEN)).astype(jnp.int32)
    return {"queries": queries, "key_states": key_states, "value_states": value_states, "grad_out": grad_out, "out_weight": out_weight, "depths": depths, "documents": documents}


def head_grads(queries, key_states, value_states, out_grad, allowed, alive_rows):
    row_count = queries.shape[0]
    head_count = queries.shape[1] // HD
    score_scale = HD ** -0.5
    query_f = queries.astype(jnp.float32).reshape(row_count, head_count, HD)
    key_f = key_states.astype(jnp.float32).reshape(row_count, head_count, HD)
    value_f = value_states.astype(jnp.float32).reshape(row_count, head_count, HD)
    grad_f = out_grad.astype(jnp.float32).reshape(row_count, head_count, HD)
    scores = jnp.einsum("qhd,khd->hqk", query_f, key_f) * score_scale
    masked = jnp.where(allowed[None], scores, -1e30)
    row_max = jnp.where(alive_rows[None, :, None], jnp.max(masked, axis=2, keepdims=True), 0.0)
    weights_raw = jnp.where(allowed[None], jnp.exp(masked - row_max), 0.0)
    row_total = jnp.sum(weights_raw, axis=2, keepdims=True)
    row_total = jnp.where(alive_rows[None, :, None], row_total, 1.0)
    probabilities = weights_raw / row_total
    probs_b = probabilities.astype(jnp.bfloat16).astype(jnp.float32)
    attended = jnp.einsum("hqk,khd->qhd", probs_b, value_f)
    row_delta = jnp.sum(grad_f * attended, axis=2)
    grad_values = jnp.einsum("hqk,qhd->khd", probs_b, grad_f)
    dprob = jnp.einsum("qhd,khd->hqk", grad_f, value_f)
    dscore = (probabilities * (dprob - row_delta.T[:, :, None])).astype(jnp.bfloat16).astype(jnp.float32)
    grad_queries = jnp.einsum("hqk,khd->qhd", dscore, key_f) * score_scale
    grad_keys = jnp.einsum("hqk,qhd->khd", dscore, query_f) * score_scale
    width = head_count * HD
    return (grad_queries.reshape(row_count, width).astype(jnp.bfloat16),
            grad_keys.reshape(row_count, width).astype(jnp.bfloat16),
            grad_values.reshape(row_count, width).astype(jnp.bfloat16))


def reference(queries, key_states, value_states, grad_out, out_weight, depths, documents):
    def one_sequence(inputs):
        query_rows, key_rows, value_rows, grad_rows, depth_row, doc_row = inputs
        out_grad = jnp.dot(grad_rows, out_weight, preferred_element_type=jnp.float32).astype(jnp.bfloat16)
        alive_rows = depth_row >= RECUR
        positions = jnp.arange(query_rows.shape[0], dtype=jnp.int32)
        allowed = (alive_rows[:, None] & alive_rows[None, :] & (doc_row[:, None] == doc_row[None, :])
                   & (positions[None, :] <= positions[:, None]))
        return head_grads(query_rows, key_rows, value_rows, out_grad, allowed, alive_rows)

    grad_queries, grad_keys, grad_values = lax.map(
        one_sequence, (queries, key_states, value_states, grad_out, depths, documents))
    return (grad_queries, grad_keys, grad_values)
```

```python
import functools

import jax
import jax.numpy as jnp
from jax import lax
from jax.experimental import pallas as pl
from jax.experimental.pallas import tpu as pltpu
from jax.sharding import PartitionSpec as P

HD = 128
RECUR = 4
GROUP = 128
CAP = 64
NX, NY, NZ = 4, 8, 8
SEQ = NX * GROUP
ROWS = NX * CAP
D = NY * NZ * 64
YB = D // NY
HALF = YB // 2
KC = D // 2
COLS = 512
HEADS = COLS // HD
VMEM = 48 * 1024 * 1024
NT = (((1,), (1,)), ((), ()))
TN = (((0,), (0,)), ((), ()))
bf16, f32 = jnp.bfloat16, jnp.float32


def _place(y, z, c):
    return ((y % NY) * NZ + z % NZ) * 2 + c


_ALL = [(y, z, c) for y in range(NY) for z in range(NZ) for c in range(2)]
Z_GROUPS = [[_place(y, z, c) for z in range(NZ)] for y in range(NY) for c in range(2)]
SWAP = [(_place(y, z, c), _place(y, z, 1 - c)) for y, z, c in _ALL]
ALONG = [(_place(y, z, c), _place(y + 1 - 2 * c, z, c)) for y, z, c in _ALL]
CROSS = [(_place(y, z, c), _place(y + 2 * c - 1, z, 1 - c)) for y, z, c in _ALL]
UP = [(i, (i + 1) % NX) for i in range(NX)]
DOWN = [(i, (i + NX - 1) % NX) for i in range(NX)]


def _dot(a, b, dims=(((1,), (0,)), ((), ()))):
    return lax.dot_general(a, b, dims, preferred_element_type=f32)


def _selection(depth_row):
    live = (depth_row >= RECUR).astype(f32)
    live8 = jnp.broadcast_to(live, (8, GROUP)).astype(bf16)
    before = (
        lax.broadcasted_iota(jnp.int32, (GROUP, GROUP), 0)
        < lax.broadcasted_iota(jnp.int32, (GROUP, GROUP), 1)
    ).astype(bf16)
    rank = _dot(live8, before)[0:1].astype(jnp.int32)
    rank = jnp.where(live > 0.0, rank, -1)
    slot = lax.broadcasted_iota(jnp.int32, (CAP, GROUP), 0)
    return (slot == rank).astype(bf16)


def _cotangent_kernel(depths_ref, grad_ref, keep_ref, send_ref):
    dp = lax.axis_index("dp")
    x = lax.axis_index("seq")
    core = lax.rem(dp, 2)
    y = lax.div(dp, 2 * NZ)
    step = 1 - 2 * core
    sel = _selection(depths_ref[:, pl.ds(pl.multiple_of(x * GROUP, GROUP), GROUP)])
    l = lax.broadcasted_iota(jnp.int32, (256, 256), 0)
    m = lax.broadcasted_iota(jnp.int32, (256, 256), 1)
    other = jnp.bitwise_xor(jnp.bitwise_and(l >> 5, 1), core)
    sort = (m == other * 128 + (l >> 6) * 32 + jnp.bitwise_and(l, 31)).astype(bf16)

    def block(index):
        index = lax.rem(index + 4 * NY, NY)
        cols = grad_ref[0, :, pl.ds(pl.multiple_of(index * YB, YB), YB)]
        rows = _dot(sel, cols).astype(bf16)
        first = _dot(rows[:, :256], sort).astype(bf16)
        second = _dot(rows[:, 256:], sort).astype(bf16)
        mine = jnp.concatenate([first[:, :128], second[:, :128]], axis=1)
        others = jnp.concatenate([first[:, 128:], second[:, 128:]], axis=1)
        return mine, others

    def put(ref, j, value):
        ref[:, j * HALF : (j + 1) * HALF] = value

    for h, j in ((0, 0), (NY // 2, 7)):
        mine, others = block(y - h)
        put(keep_ref, j, mine)
        put(send_ref, j, others)
    for h in range(1, NY // 2):
        mine, others = block(y - h * step)
        put(keep_ref, 2 * h - 1, mine)
        put(keep_ref, 2 * h, others)
        mine, others = block(y + h * step)
        put(send_ref, 2 * h - 1, others)
        put(send_ref, 2 * h, mine)


def _softmax_kernel(
    depths_ref, documents_ref, q_ref, k_ref, v_ref, qc_ref, kc_ref, vc_ref, probs_ref, attended_ref, sel_ref
):
    docs_col, docs_row, valid_col, valid_row = [], [], [], []
    for b in range(NX):
        at = slice(b * GROUP, (b + 1) * GROUP)
        to = slice(b * CAP, (b + 1) * CAP)
        sel = _selection(depths_ref[:, at])
        sel_ref[to, :] = sel
        for src, dst in ((q_ref, qc_ref), (k_ref, kc_ref), (v_ref, vc_ref)):
            dst[to, :] = _dot(sel, src[0, at, :]).astype(bf16)
        docs = documents_ref[:, at].astype(f32)
        docs8 = jnp.broadcast_to(docs, (8, GROUP)).astype(bf16)
        ones8 = jnp.ones((8, GROUP), bf16)
        picked = sel.astype(f32)
        docs_col.append(jnp.sum(picked * docs, axis=1, keepdims=True))
        valid_col.append(jnp.sum(picked, axis=1, keepdims=True))
        docs_row.append(_dot(docs8, sel, NT)[0:1])
        valid_row.append(_dot(ones8, sel, NT)[0:1])
    doc_c = jnp.concatenate(docs_col, axis=0)
    doc_r = jnp.concatenate(docs_row, axis=1)
    val_c = jnp.concatenate(valid_col, axis=0)
    val_r = jnp.concatenate(valid_row, axis=1)
    doc_c = jnp.where(val_c > 0.5, doc_c, -1.0)
    doc_r = jnp.where(val_r > 0.5, doc_r, -2.0)
    i = lax.broadcasted_iota(jnp.int32, (ROWS, ROWS), 0)
    j = lax.broadcasted_iota(jnp.int32, (ROWS, ROWS), 1)
    allowed = (doc_c == doc_r) & (j <= i)
    scale = HD ** (-0.5)
    for h in range(HEADS):
        cols = slice(h * HD, (h + 1) * HD)
        scores = _dot(qc_ref[:, cols], kc_ref[:, cols], NT) * scale
        masked = jnp.where(allowed, scores, -1e30)
        top = jnp.max(masked, axis=1, keepdims=True)
        raw = jnp.where(allowed, jnp.exp(masked - top), 0.0)
        total = jnp.sum(raw, axis=1, keepdims=True)
        total = jnp.where(total > 0.0, total, 1.0)
        probs = raw * (1.0 / total)
        probs_ref[h] = probs
        attended_ref[:, cols] = _dot(probs.astype(bf16), vc_ref[:, cols])


def _project_kernel(
    own_ref, hop1_ref, hop2_ref, hop3_ref, hop4_ref, g0_ref, g1_ref, g3_ref, g2a_ref, g2b_ref, mine_ref, other_ref
):
    x = lax.axis_index("seq")

    def rows_at(shift):
        return pl.ds(pl.multiple_of(lax.rem(x + shift + NX, NX) * CAP, CAP), CAP)

    pieces = (
        (g0_ref, slice(0, CAP), mine_ref, 0),
        (g0_ref, slice(CAP, 2 * CAP), other_ref, 0),
        (g1_ref, slice(0, CAP), mine_ref, -1),
        (g1_ref, slice(CAP, 2 * CAP), other_ref, -1),
        (g3_ref, slice(0, CAP), mine_ref, 1),
        (g3_ref, slice(CAP, 2 * CAP), other_ref, 1),
        (g2a_ref, slice(0, CAP), mine_ref, 2),
        (g2b_ref, slice(0, CAP), other_ref, 2),
    )
    weights = (
        (own_ref, 0, HALF),
        (hop1_ref, HALF, 2 * HALF),
        (hop2_ref, 3 * HALF, 2 * HALF),
        (hop3_ref, 5 * HALF, 2 * HALF),
        (hop4_ref, 7 * HALF, HALF),
    )
    rows = jnp.concatenate([g[at, :] for g, at, _, _ in pieces], axis=0)
    total = None
    for w, k, n in weights:
        term = _dot(rows[:, k : k + n], w[...])
        total = term if total is None else total + term
    for n, (_, _, out, shift) in enumerate(pieces):
        out[rows_at(shift), :] = total[n * CAP : (n + 1) * CAP]


def _gradients_kernel(
    mine_ref, other_ref, qc_ref, kc_ref, vc_ref, probs_ref, attended_ref, sel_ref, dq_ref, dk_ref, dv_ref
):
    scale = HD ** (-0.5)
    for h in range(HEADS):
        cols = slice(h * HD, (h + 1) * HD)
        out_grad = (mine_ref[:, cols] + other_ref[:, cols]).astype(bf16)
        q, k, v = qc_ref[:, cols], kc_ref[:, cols], vc_ref[:, cols]
        probs = probs_ref[h]
        delta = jnp.sum(out_grad.astype(f32) * attended_ref[:, cols], axis=1, keepdims=True)
        dscore = (probs * (_dot(out_grad, v, NT) - delta)).astype(bf16)
        dv = _dot(probs.astype(bf16), out_grad, TN).astype(bf16)
        dq = (_dot(dscore, k) * scale).astype(bf16)
        dk = (_dot(dscore, q, TN) * scale).astype(bf16)
        for b in range(NX):
            at = slice(b * GROUP, (b + 1) * GROUP)
            frm = slice(b * CAP, (b + 1) * CAP)
            sel = sel_ref[frm, :]
            for src, dst in ((dq, dq_ref), (dk, dk_ref), (dv, dv_ref)):
                dst[0, at, cols] = _dot(sel, src[frm, :], TN).astype(bf16)


def _call(kernel, outs, flops, nbytes, exps=0):
    return pl.pallas_call(
        kernel,
        out_shape=tuple(jax.ShapeDtypeStruct(s, t) for s, t in outs),
        compiler_params=pltpu.CompilerParams(vmem_limit_bytes=VMEM),
        cost_estimate=pl.CostEstimate(flops=flops, bytes_accessed=nbytes, transcendentals=exps),
    )


def on_device(queries, key_states, value_states, grad_out, out_weight, depths, documents):
    copies = jnp.broadcast_to(out_weight[None], (NZ,) + out_weight.shape)
    own = lax.all_to_all(copies, "dp", 0, 0, axis_index_groups=Z_GROUPS).reshape(HALF, COLS)
    keep, send = _call(
        _cotangent_kernel, [((CAP, KC), bf16)] * 2, 2 * CAP * D * (GROUP + 256), 2 << 20
    )(depths, grad_out)
    got = lax.ppermute(send, "dp", SWAP)
    g0 = jnp.concatenate([keep, got], axis=0)
    g1 = lax.ppermute(g0, "seq", UP)
    g3 = lax.ppermute(g0, "seq", DOWN)
    g2a = lax.ppermute(g1[:CAP], "seq", UP)
    g2b = lax.ppermute(g3[CAP:], "seq", DOWN)
    hop1 = jnp.concatenate([lax.ppermute(own, "dp", ALONG), lax.ppermute(own, "dp", CROSS)], axis=0)
    hop2 = lax.ppermute(hop1, "dp", ALONG)
    hop3 = lax.ppermute(hop2, "dp", ALONG)
    hop4 = lax.ppermute(hop3[:HALF], "dp", ALONG)
    qc, kc, vc, probs, attended, sel = _call(
        _softmax_kernel,
        [((ROWS, COLS), bf16)] * 3
        + [((HEADS, ROWS, ROWS), f32), ((ROWS, COLS), f32), ((ROWS, GROUP), bf16)],
        4 * HEADS * ROWS * ROWS * HD,
        4 << 20,
        HEADS * ROWS * ROWS,
    )(depths, documents, queries, key_states, value_states)
    mine, other = _call(
        _project_kernel, [((ROWS, COLS), f32)] * 2, 4 * ROWS * KC * COLS, 5 << 20
    )(own, hop1, hop2, hop3, hop4, g0, g1, g3, g2a, g2b)
    theirs = lax.ppermute(other, "dp", SWAP)
    return _call(
        _gradients_kernel, [((1, SEQ, COLS), bf16)] * 3, 10 * HEADS * ROWS * ROWS * HD, 5 << 20
    )(mine, theirs, qc, kc, vc, probs, attended, sel)


def solution(mesh):
    return jax.shard_map(
        on_device,
        mesh=mesh,
        in_specs=(
            P("dp", None, "seq"),
            P("dp", None, "seq"),
            P("dp", None, "seq"),
            P("dp", "seq", None),
            P("dp", "seq"),
            P("dp", None),
            P("dp", None),
        ),
        out_specs=(P("dp", None, "seq"), P("dp", None, "seq"), P("dp", None, "seq")),
        check_vma=False,
    )
```

```python
import functools

import jax
import jax.numpy as jnp
from jax import lax
from jax.experimental import pallas as pl
from jax.experimental.pallas import tpu as pltpu
from jax.sharding import PartitionSpec as P

HD = 128
RECUR = 4
GROUP = 128
CAP = 64
NX, NY, NZ = 4, 8, 8
SEQ = NX * GROUP
ROWS = NX * CAP
D = NY * NZ * 64
YB = D // NY
HALF = YB // 2
KC = D // 2
COLS = 512
HEADS = COLS // HD
VMEM = 48 * 1024 * 1024
NT = (((1,), (1,)), ((), ()))
TN = (((0,), (0,)), ((), ()))
bf16, f32 = jnp.bfloat16, jnp.float32


def _place(y, z, c):
    return ((y % NY) * NZ + z % NZ) * 2 + c


_ALL = [(y, z, c) for y in range(NY) for z in range(NZ) for c in range(2)]
Z_GROUPS = [[_place(y, z, c) for z in range(NZ)] for y in range(NY) for c in range(2)]
SWAP = [(_place(y, z, c), _place(y, z, 1 - c)) for y, z, c in _ALL]
Y_FIRST = [
    (_place(y, z, c), _place(y + 1 - 2 * (c ^ (z & 1)), z, c ^ (z & 1))) for y, z, c in _ALL
]
Y_ALONG = [(_place(y, z, c), _place(y + 1 - 2 * c, z, c)) for y, z, c in _ALL]
Z_SWAP = [(_place(y, z, c), _place(y, z ^ 1, c)) for y, z, c in _ALL]
X_ALONG, X_AGAINST = (
    [
        (_place(y, z, c) * NX + x, _place(y, z, c) * NX + (x + way * (1 - 2 * c)) % NX)
        for y, z, c in _ALL
        for x in range(NX)
    ]
    for way in (1, -1)
)


def _dot(a, b, dims=(((1,), (0,)), ((), ()))):
    return lax.dot_general(a, b, dims, preferred_element_type=f32)


def _selection(depth_row):
    live = (depth_row >= RECUR).astype(f32)
    live8 = jnp.broadcast_to(live, (8, GROUP)).astype(bf16)
    before = (
        lax.broadcasted_iota(jnp.int32, (GROUP, GROUP), 0)
        < lax.broadcasted_iota(jnp.int32, (GROUP, GROUP), 1)
    ).astype(bf16)
    rank = _dot(live8, before)[0:1].astype(jnp.int32)
    rank = jnp.where(live > 0.0, rank, -1)
    slot = lax.broadcasted_iota(jnp.int32, (CAP, GROUP), 0)
    return (slot == rank).astype(bf16)


def _cotangent_kernel(depths_ref, grad_ref, keep_ref, send_ref, q_ref, o_ref):
    dp = lax.axis_index("dp")
    x = lax.axis_index("seq")
    core = lax.rem(dp, 2)
    odd = lax.rem(lax.div(dp, 2), 2)
    y = lax.div(dp, 2 * NZ)
    step = 1 - 2 * core
    sel = _selection(depths_ref[:, pl.ds(pl.multiple_of(x * GROUP, GROUP), GROUP)])
    l = lax.broadcasted_iota(jnp.int32, (256, 256), 0)
    m = lax.broadcasted_iota(jnp.int32, (256, 256), 1)
    other = jnp.bitwise_xor(jnp.bitwise_and(l >> 5, 1), jnp.bitwise_xor(core, odd))
    sort = (m == other * 128 + (l >> 6) * 32 + jnp.bitwise_and(l, 31)).astype(bf16)
    rows = _dot(sel, grad_ref[0]).astype(bf16)
    for n in range(D // 256):
        at = slice(n * 128, (n + 1) * 128)
        pair = _dot(rows[:, n * 256 : (n + 1) * 256], sort).astype(bf16)
        q_ref[:, at] = pair[:, :128]
        o_ref[:, at] = pair[:, 128:]

    def block(ref, index):
        index = lax.rem(index + 4 * NY, NY)
        return ref[:, pl.ds(pl.multiple_of(index * HALF, HALF), HALF)]

    def put(ref, j, value):
        ref[:, j * HALF : (j + 1) * HALF] = value

    own_q, own_o = block(q_ref, y), block(o_ref, y)
    put(keep_ref, 0, jnp.where(odd == 0, own_q, own_o))
    put(send_ref, 0, jnp.where(odd == 0, own_o, own_q))
    put(keep_ref, 7, block(q_ref, y + NY // 2))
    put(send_ref, 7, block(o_ref, y + NY // 2))
    for h in range(1, NY // 2):
        put(keep_ref, 2 * h - 1, block(q_ref, y - h * step))
        put(keep_ref, 2 * h, block(o_ref, y - h * step))
        put(send_ref, 2 * h - 1, block(o_ref, y + h * step))
        put(send_ref, 2 * h, block(q_ref, y + h * step))


def _softmax_kernel(
    depths_ref, documents_ref, q_ref, k_ref, v_ref, qc_ref, kc_ref, vc_ref, probs_ref, attended_ref, sel_ref
):
    docs_col, docs_row, valid_col, valid_row = [], [], [], []
    for b in range(NX):
        at = slice(b * GROUP, (b + 1) * GROUP)
        to = slice(b * CAP, (b + 1) * CAP)
        sel = _selection(depths_ref[:, at])
        sel_ref[to, :] = sel
        for src, dst in ((q_ref, qc_ref), (k_ref, kc_ref), (v_ref, vc_ref)):
            dst[to, :] = _dot(sel, src[0, at, :]).astype(bf16)
        docs = documents_ref[:, at].astype(f32)
        docs8 = jnp.broadcast_to(docs, (8, GROUP)).astype(bf16)
        ones8 = jnp.ones((8, GROUP), bf16)
        picked = sel.astype(f32)
        docs_col.append(jnp.sum(picked * docs, axis=1, keepdims=True))
        valid_col.append(jnp.sum(picked, axis=1, keepdims=True))
        docs_row.append(_dot(docs8, sel, NT)[0:1])
        valid_row.append(_dot(ones8, sel, NT)[0:1])
    doc_c = jnp.concatenate(docs_col, axis=0)
    doc_r = jnp.concatenate(docs_row, axis=1)
    val_c = jnp.concatenate(valid_col, axis=0)
    val_r = jnp.concatenate(valid_row, axis=1)
    doc_c = jnp.where(val_c > 0.5, doc_c, -1.0)
    doc_r = jnp.where(val_r > 0.5, doc_r, -2.0)
    i = lax.broadcasted_iota(jnp.int32, (ROWS, ROWS), 0)
    j = lax.broadcasted_iota(jnp.int32, (ROWS, ROWS), 1)
    allowed = (doc_c == doc_r) & (j <= i)
    scale = HD ** (-0.5)
    for h in range(HEADS):
        cols = slice(h * HD, (h + 1) * HD)
        scores = _dot(qc_ref[:, cols], kc_ref[:, cols], NT) * scale
        masked = jnp.where(allowed, scores, -1e30)
        top = jnp.max(masked, axis=1, keepdims=True)
        raw = jnp.where(allowed, jnp.exp(masked - top), 0.0)
        total = jnp.sum(raw, axis=1, keepdims=True)
        total = jnp.where(total > 0.0, total, 1.0)
        probs = raw * (1.0 / total)
        probs_ref[h] = probs
        attended_ref[:, cols] = _dot(probs.astype(bf16), vc_ref[:, cols])


def _partial(g_refs, w_refs, start):
    total = None
    for n, w_ref in enumerate(w_refs):
        cols = slice(start + n * HALF, start + (n + 1) * HALF)
        term = _dot(jnp.concatenate([g[:, cols] for g in g_refs], axis=0), w_ref[...])
        total = term if total is None else total + term
    return total


def _project_first_kernel(own_ref, a1_ref, b1_ref, a2_ref, b2_ref, g0_ref, g1_ref, g2_ref, g3_ref, out_ref):
    out_ref[...] = _partial(
        (g0_ref, g1_ref, g2_ref, g3_ref), (own_ref, a1_ref, b1_ref, a2_ref, b2_ref), 0
    )


def _project_last_kernel(
    first_ref, a3_ref, b3_ref, a4_ref, g0_ref, g1_ref, g2_ref, g3_ref, mine_ref, other_ref
):
    x = lax.axis_index("seq")
    step = 1 - 2 * lax.rem(lax.axis_index("dp"), 2)
    total = first_ref[...] + _partial(
        (g0_ref, g1_ref, g2_ref, g3_ref), (a3_ref, b3_ref, a4_ref), 5 * HALF
    )
    for n, shift in enumerate((0, -step, 2, step)):
        at = pl.ds(pl.multiple_of(lax.rem(x + shift + NX, NX) * CAP, CAP), CAP)
        mine_ref[at, :] = total[2 * n * CAP : (2 * n + 1) * CAP]
        other_ref[at, :] = total[(2 * n + 1) * CAP : (2 * n + 2) * CAP]


def _gradients_kernel(
    mine_ref, other_ref, qc_ref, kc_ref, vc_ref, probs_ref, attended_ref, sel_ref, dq_ref, dk_ref, dv_ref
):
    scale = HD ** (-0.5)
    for h in range(HEADS):
        cols = slice(h * HD, (h + 1) * HD)
        out_grad = (mine_ref[:, cols] + other_ref[:, cols]).astype(bf16)
        q, k, v = qc_ref[:, cols], kc_ref[:, cols], vc_ref[:, cols]
        probs = probs_ref[h]
        delta = jnp.sum(out_grad.astype(f32) * attended_ref[:, cols], axis=1, keepdims=True)
        dscore = (probs * (_dot(out_grad, v, NT) - delta)).astype(bf16)
        dv = _dot(probs.astype(bf16), out_grad, TN).astype(bf16)
        dq = (_dot(dscore, k) * scale).astype(bf16)
        dk = (_dot(dscore, q, TN) * scale).astype(bf16)
        for b in range(NX):
            at = slice(b * GROUP, (b + 1) * GROUP)
            frm = slice(b * CAP, (b + 1) * CAP)
            sel = sel_ref[frm, :]
            for src, dst in ((dq, dq_ref), (dk, dk_ref), (dv, dv_ref)):
                dst[0, at, cols] = _dot(sel, src[frm, :], TN).astype(bf16)


def _call(kernel, outs, flops, nbytes, exps=0, scratch=()):
    return pl.pallas_call(
        kernel,
        out_shape=tuple(jax.ShapeDtypeStruct(s, t) for s, t in outs),
        scratch_shapes=scratch,
        compiler_params=pltpu.CompilerParams(vmem_limit_bytes=VMEM),
        cost_estimate=pl.CostEstimate(flops=flops, bytes_accessed=nbytes, transcendentals=exps),
    )


def on_device(queries, key_states, value_states, grad_out, out_weight, depths, documents):
    keep, send = _call(
        _cotangent_kernel,
        [((CAP, KC), bf16)] * 2,
        2 * CAP * D * (GROUP + 256),
        2 << 20,
        scratch=[pltpu.VMEM((CAP, KC), bf16)] * 2,
    )(depths, grad_out)
    got = lax.ppermute(send, "dp", SWAP)
    g0 = jnp.concatenate([keep, got], axis=0)
    copies = jnp.broadcast_to(out_weight[None], (NZ,) + out_weight.shape)
    own = lax.all_to_all(copies, "dp", 0, 0, axis_index_groups=Z_GROUPS).reshape(HALF, COLS)
    g1 = lax.ppermute(g0, ("dp", "seq"), X_ALONG)
    g3 = lax.ppermute(g0, ("dp", "seq"), X_AGAINST)
    g2 = lax.ppermute(g1, ("dp", "seq"), X_ALONG)
    a1 = lax.ppermute(own, "dp", Y_FIRST)
    a1, g1 = lax.optimization_barrier((a1, g1))
    a2 = lax.ppermute(a1, "dp", Y_ALONG)
    b1 = lax.ppermute(a1, "dp", Z_SWAP)
    a2, g3 = lax.optimization_barrier((a2, g3))
    a3 = lax.ppermute(a2, "dp", Y_ALONG)
    b2 = lax.ppermute(a2, "dp", Z_SWAP)
    a3, b1, g2 = lax.optimization_barrier((a3, b1, g2))
    a4 = lax.ppermute(a3, "dp", Y_ALONG)
    b3 = lax.ppermute(a3, "dp", Z_SWAP)
    qc, kc, vc, probs, attended, sel = _call(
        _softmax_kernel,
        [((ROWS, COLS), bf16)] * 3
        + [((HEADS, ROWS, ROWS), f32), ((ROWS, COLS), f32), ((ROWS, GROUP), bf16)],
        4 * HEADS * ROWS * ROWS * HD,
        4 << 20,
        HEADS * ROWS * ROWS,
    )(depths, documents, queries, key_states, value_states)
    first = _call(
        _project_first_kernel, [((2 * ROWS, COLS), f32)], 20 * ROWS * HALF * COLS, 5 << 20
    )(own, a1, b1, a2, b2, g0, g1, g2, g3)[0]
    mine, other = _call(
        _project_last_kernel, [((ROWS, COLS), f32)] * 2, 12 * ROWS * HALF * COLS, 5 << 20
    )(first, a3, b3, a4, g0, g1, g2, g3)
    theirs = lax.ppermute(other, "dp", SWAP)
    return _call(
        _gradients_kernel, [((1, SEQ, COLS), bf16)] * 3, 10 * HEADS * ROWS * ROWS * HD, 5 << 20
    )(mine, theirs, qc, kc, vc, probs, attended, sel)


def solution(mesh):
    return jax.shard_map(
        on_device,
        mesh=mesh,
        in_specs=(
            P("dp", None, "seq"),
            P("dp", None, "seq"),
            P("dp", None, "seq"),
            P("dp", "seq", None),
            P("dp", "seq"),
            P("dp", None),
            P("dp", None),
        ),
        out_specs=(P("dp", None, "seq"), P("dp", None, "seq"), P("dp", None, "seq")),
        check_vma=False,
    )
```

```python
import functools

import jax
import jax.numpy as jnp
from jax import lax
from jax.experimental import pallas as pl
from jax.experimental.pallas import tpu as pltpu
from jax.sharding import PartitionSpec as P

HD = 128
RECUR = 4
GROUP = 128
CAP = 64
NX, NY, NZ = 4, 8, 8
SEQ = NX * GROUP
ROWS = NX * CAP
D = NY * NZ * 64
YB = D // NY
HALF = YB // 2
KC = D // 2
COLS = 512
HEADS = COLS // HD
VMEM = 48 * 1024 * 1024
PREP_VMEM = 60 * 1024 * 1024
NT = (((1,), (1,)), ((), ()))
TN = (((0,), (0,)), ((), ()))
bf16, f32 = jnp.bfloat16, jnp.float32
SENT = bf16


def _place(y, z, c):
    return ((y % NY) * NZ + z % NZ) * 2 + c


_ALL = [(y, z, c) for y in range(NY) for z in range(NZ) for c in range(2)]
Z_GROUPS = [[_place(y, z, c) for z in range(NZ)] for y in range(NY) for c in range(2)]
SWAP = [(_place(y, z, c), _place(y, z, 1 - c)) for y, z, c in _ALL]
Y_FIRST = [
    (_place(y, z, c), _place(y + 1 - 2 * (c ^ (z & 1)), z, c ^ (z & 1))) for y, z, c in _ALL
]
Y_ALONG = [(_place(y, z, c), _place(y + 1 - 2 * c, z, c)) for y, z, c in _ALL]
Z_SWAP = [(_place(y, z, c), _place(y, z ^ 1, c)) for y, z, c in _ALL]
X_ALONG, X_AGAINST = (
    [
        (_place(y, z, c) * NX + x, _place(y, z, c) * NX + (x + way * (1 - 2 * c)) % NX)
        for y, z, c in _ALL
        for x in range(NX)
    ]
    for way in (1, -1)
)


def _dot(a, b, dims=(((1,), (0,)), ((), ()))):
    return lax.dot_general(a, b, dims, preferred_element_type=f32)


def _selection(depth_row):
    live = (depth_row >= RECUR).astype(f32)
    live8 = jnp.broadcast_to(live, (8, GROUP)).astype(bf16)
    before = (
        lax.broadcasted_iota(jnp.int32, (GROUP, GROUP), 0)
        < lax.broadcasted_iota(jnp.int32, (GROUP, GROUP), 1)
    ).astype(bf16)
    rank = _dot(live8, before)[0:1].astype(jnp.int32)
    rank = jnp.where(live > 0.0, rank, -1)
    slot = lax.broadcasted_iota(jnp.int32, (CAP, GROUP), 0)
    return (slot == rank).astype(bf16)


def _prepare_kernel(
    depths_any, grad_any, weight_any, copies_ref, keep_ref, send_ref, q_ref, o_ref, depths_ref, grad_ref, weight_ref, sems
):
    loads = [
        pltpu.make_async_copy(depths_any, depths_ref, sems.at[0]),
        pltpu.make_async_copy(weight_any, weight_ref, sems.at[1]),
        pltpu.make_async_copy(grad_any, grad_ref, sems.at[2]),
    ]
    for load in loads:
        load.start()
    dp = lax.axis_index("dp")
    x = lax.axis_index("seq")
    core = lax.rem(dp, 2)
    odd = lax.rem(lax.div(dp, 2), 2)
    y = lax.div(dp, 2 * NZ)
    step = 1 - 2 * core
    l = lax.broadcasted_iota(jnp.int32, (256, 256), 0)
    m = lax.broadcasted_iota(jnp.int32, (256, 256), 1)
    other = jnp.bitwise_xor(jnp.bitwise_and(l >> 5, 1), jnp.bitwise_xor(core, odd))
    sort = (m == other * 128 + (l >> 6) * 32 + jnp.bitwise_and(l, 31)).astype(bf16)
    loads[0].wait()
    sel = _selection(depths_ref[:, pl.ds(pl.multiple_of(x * GROUP, GROUP), GROUP)])
    loads[1].wait()
    for z in range(NZ):
        copies_ref[z] = weight_ref[...]
    loads[2].wait()
    rows = _dot(sel, grad_ref[0]).astype(bf16)
    for n in range(D // 256):
        at = slice(n * 128, (n + 1) * 128)
        pair = _dot(rows[:, n * 256 : (n + 1) * 256], sort).astype(bf16)
        q_ref[:, at] = pair[:, :128]
        o_ref[:, at] = pair[:, 128:]

    def block(ref, index):
        index = lax.rem(index + 4 * NY, NY)
        return ref[:, pl.ds(pl.multiple_of(index * HALF, HALF), HALF)]

    def put(ref, j, value):
        ref[:, j * HALF : (j + 1) * HALF] = value

    own_q, own_o = block(q_ref, y), block(o_ref, y)
    put(keep_ref, 0, jnp.where(odd == 0, own_q, own_o))
    put(send_ref, 0, jnp.where(odd == 0, own_o, own_q))
    put(keep_ref, 7, block(q_ref, y + NY // 2))
    put(send_ref, 7, block(o_ref, y + NY // 2))
    for h in range(1, NY // 2):
        put(keep_ref, 2 * h - 1, block(q_ref, y - h * step))
        put(keep_ref, 2 * h, block(o_ref, y - h * step))
        put(send_ref, 2 * h - 1, block(o_ref, y + h * step))
        put(send_ref, 2 * h, block(q_ref, y + h * step))


def _softmax_kernel(
    depths_ref, documents_ref, q_ref, k_ref, v_ref, qc_ref, kc_ref, vc_ref, probs_ref, turned_ref, attended_ref, place_ref
):
    docs_col, docs_row, valid_col, valid_row = [], [], [], []
    for b in range(NX):
        at = slice(b * GROUP, (b + 1) * GROUP)
        to = slice(b * CAP, (b + 1) * CAP)
        sel = _selection(depths_ref[:, at])
        place_ref[at, :] = sel.astype(f32).T.astype(bf16)
        for src, dst in ((q_ref, qc_ref), (k_ref, kc_ref), (v_ref, vc_ref)):
            dst[to, :] = _dot(sel, src[0, at, :]).astype(bf16)
        docs = documents_ref[:, at].astype(f32)
        docs8 = jnp.broadcast_to(docs, (8, GROUP)).astype(bf16)
        ones8 = jnp.ones((8, GROUP), bf16)
        picked = sel.astype(f32)
        docs_col.append(jnp.sum(picked * docs, axis=1, keepdims=True))
        valid_col.append(jnp.sum(picked, axis=1, keepdims=True))
        docs_row.append(_dot(docs8, sel, NT)[0:1])
        valid_row.append(_dot(ones8, sel, NT)[0:1])
    doc_c = jnp.concatenate(docs_col, axis=0)
    doc_r = jnp.concatenate(docs_row, axis=1)
    val_c = jnp.concatenate(valid_col, axis=0)
    val_r = jnp.concatenate(valid_row, axis=1)
    doc_c = jnp.where(val_c > 0.5, doc_c, -1.0)
    doc_r = jnp.where(val_r > 0.5, doc_r, -2.0)
    i = lax.broadcasted_iota(jnp.int32, (ROWS, ROWS), 0)
    j = lax.broadcasted_iota(jnp.int32, (ROWS, ROWS), 1)
    allowed = (doc_c == doc_r) & (j <= i)
    scale = HD ** (-0.5)
    for h in range(HEADS):
        cols = slice(h * HD, (h + 1) * HD)
        scores = _dot(qc_ref[:, cols], kc_ref[:, cols], NT) * scale
        masked = jnp.where(allowed, scores, -1e30)
        top = jnp.max(masked, axis=1, keepdims=True)
        raw = jnp.where(allowed, jnp.exp(masked - top), 0.0)
        total = jnp.sum(raw, axis=1, keepdims=True)
        total = jnp.where(total > 0.0, total, 1.0)
        probs = raw * (1.0 / total)
        probs_ref[h] = probs
        turned_ref[h] = probs.T.astype(bf16)
        attended_ref[:, cols] = _dot(probs.astype(bf16), vc_ref[:, cols])


def _partial(g_refs, w_refs, start):
    total = None
    for n, w_ref in enumerate(w_refs):
        cols = slice(start + n * HALF, start + (n + 1) * HALF)
        term = _dot(jnp.concatenate([g[:, cols] for g in g_refs], axis=0), w_ref[...])
        total = term if total is None else total + term
    return total


def _project_first_kernel(own_ref, a1_ref, b1_ref, a2_ref, b2_ref, g0_ref, g1_ref, g2_ref, g3_ref, out_ref):
    out_ref[...] = _partial(
        (g0_ref, g1_ref, g2_ref, g3_ref), (own_ref, a1_ref, b1_ref, a2_ref, b2_ref), 0
    )


def _project_last_kernel(own, first_ref, a3_ref, b3_ref, a4_ref, g0_ref, g1_ref, g2_ref, g3_ref, out_ref):
    x = lax.axis_index("seq")
    step = 1 - 2 * lax.rem(lax.axis_index("dp"), 2)
    part = slice(0, CAP) if own else slice(CAP, 2 * CAP)
    gs = [g.at[part] for g in (g0_ref, g1_ref, g2_ref, g3_ref)]
    total = _partial(gs, (a3_ref, b3_ref, a4_ref), 5 * HALF)
    for n, shift in enumerate((0, -step, 2, step)):
        at = pl.ds(pl.multiple_of(lax.rem(x + shift + NX, NX) * CAP, CAP), CAP)
        frm = slice(2 * n * CAP + part.start, 2 * n * CAP + part.stop)
        out_ref[at, :] = (total[n * CAP : (n + 1) * CAP] + first_ref[frm, :]).astype(out_ref.dtype)


def _gradients_kernel(
    mine_ref, other_ref, qc_ref, kc_ref, vc_ref, probs_ref, turned_ref, attended_ref, place_ref,
    dq_any, dk_any, dv_any, og_ref, rows_ref, dq_ref, dk_ref, dv_ref, sems,
):
    scale = HD ** (-0.5)
    og_ref[...] = (mine_ref[...] + other_ref[...].astype(f32)).astype(bf16)
    heads = [slice(h * HD, (h + 1) * HD) for h in range(HEADS)]

    def finish(n, full_ref, out_any):
        for b in range(NX):
            at = slice(b * GROUP, (b + 1) * GROUP)
            full_ref[0, at, :] = _dot(place_ref[at, :], rows_ref[n, b * CAP : (b + 1) * CAP, :]).astype(bf16)
        copy = pltpu.make_async_copy(full_ref, out_any, sems.at[n])
        copy.start()
        return copy

    for h, cols in enumerate(heads):
        rows_ref[2, :, cols] = _dot(turned_ref[h], og_ref[:, cols]).astype(bf16)
    copies = [finish(2, dv_ref, dv_any)]
    dscores = []
    for h, cols in enumerate(heads):
        out_grad = og_ref[:, cols]
        delta = jnp.sum(out_grad.astype(f32) * attended_ref[:, cols], axis=1, keepdims=True)
        dscore = (probs_ref[h] * (_dot(out_grad, vc_ref[:, cols], NT) - delta)).astype(bf16)
        rows_ref[0, :, cols] = (_dot(dscore, kc_ref[:, cols]) * scale).astype(bf16)
        dscores.append(dscore)
    copies.append(finish(0, dq_ref, dq_any))
    for h, cols in enumerate(heads):
        rows_ref[1, :, cols] = (_dot(dscores[h], qc_ref[:, cols], TN) * scale).astype(bf16)
    copies.append(finish(1, dk_ref, dk_any))
    for copy in copies:
        copy.wait()


def _call(kernel, outs, flops, nbytes, exps=0, scratch=(), vmem=VMEM, **specs):
    return pl.pallas_call(
        kernel,
        out_shape=tuple(jax.ShapeDtypeStruct(s, t) for s, t in outs),
        scratch_shapes=scratch,
        **specs,
        compiler_params=pltpu.CompilerParams(vmem_limit_bytes=vmem),
        cost_estimate=pl.CostEstimate(flops=flops, bytes_accessed=nbytes, transcendentals=exps),
    )


def on_device(queries, key_states, value_states, grad_out, out_weight, depths, documents):
    copies, keep, send = _call(
        _prepare_kernel,
        [((NZ, D // (NY * NZ * 2), COLS), bf16)] + [((CAP, KC), bf16)] * 2,
        2 * CAP * D * (GROUP + 256),
        2 << 20,
        scratch=[pltpu.VMEM((CAP, KC), bf16)] * 2
        + [
            pltpu.VMEM((1, SEQ), jnp.int32),
            pltpu.VMEM((1, GROUP, D), bf16),
            pltpu.VMEM((D // (NY * NZ * 2), COLS), bf16),
            pltpu.SemaphoreType.DMA((3,)),
        ],
        vmem=PREP_VMEM,
        in_specs=[pl.BlockSpec(memory_space=pl.ANY)] * 3,
    )(depths, grad_out, out_weight)
    got = lax.ppermute(send, "dp", SWAP)
    g0 = jnp.concatenate([keep, got], axis=0)
    own = lax.all_to_all(copies, "dp", 0, 0, axis_index_groups=Z_GROUPS).reshape(HALF, COLS)
    g1 = lax.ppermute(g0, ("dp", "seq"), X_ALONG)
    g3 = lax.ppermute(g0, ("dp", "seq"), X_AGAINST)
    g2 = lax.ppermute(g1, ("dp", "seq"), X_ALONG)
    a1 = lax.ppermute(own, "dp", Y_FIRST)
    a1, g1 = lax.optimization_barrier((a1, g1))
    a2 = lax.ppermute(a1, "dp", Y_ALONG)
    b1 = lax.ppermute(a1, "dp", Z_SWAP)
    a2, g3 = lax.optimization_barrier((a2, g3))
    a3 = lax.ppermute(a2, "dp", Y_ALONG)
    b2 = lax.ppermute(a2, "dp", Z_SWAP)
    a3, b1, g2 = lax.optimization_barrier((a3, b1, g2))
    a4 = lax.ppermute(a3, "dp", Y_ALONG)
    b3 = lax.ppermute(a3, "dp", Z_SWAP)
    qc, kc, vc, probs, turned, attended, place = _call(
        _softmax_kernel,
        [((ROWS, COLS), bf16)] * 3
        + [((HEADS, ROWS, ROWS), f32), ((HEADS, ROWS, ROWS), bf16), ((ROWS, COLS), f32), ((SEQ, CAP), bf16)],
        4 * HEADS * ROWS * ROWS * HD,
        4 << 20,
        HEADS * ROWS * ROWS,
    )(depths, documents, queries, key_states, value_states)
    first = _call(
        _project_first_kernel, [((2 * ROWS, COLS), f32)], 20 * ROWS * HALF * COLS, 5 << 20
    )(own, a1, b1, a2, b2, g0, g1, g2, g3)[0]
    first, probs = lax.optimization_barrier((first, probs))
    last = (first, a3, b3, a4, g0, g1, g2, g3)
    other = _call(
        functools.partial(_project_last_kernel, False), [((ROWS, COLS), SENT)], 6 * ROWS * HALF * COLS, 3 << 20
    )(*last)[0]
    swapped = lax.ppermute(other, "dp", SWAP)
    mine = _call(
        functools.partial(_project_last_kernel, True), [((ROWS, COLS), f32)], 6 * ROWS * HALF * COLS, 3 << 20
    )(*last)[0]
    return _call(
        _gradients_kernel,
        [((1, SEQ, COLS), bf16)] * 3,
        10 * HEADS * ROWS * ROWS * HD,
        5 << 20,
        scratch=[pltpu.VMEM((ROWS, COLS), bf16), pltpu.VMEM((3, ROWS, COLS), bf16)]
        + [pltpu.VMEM((1, SEQ, COLS), bf16)] * 3
        + [pltpu.SemaphoreType.DMA((3,))],
        out_specs=tuple([pl.BlockSpec(memory_space=pl.ANY)] * 3),
    )(mine, swapped, qc, kc, vc, probs, turned, attended, place)


def solution(mesh):
    return jax.shard_map(
        on_device,
        mesh=mesh,
        in_specs=(
            P("dp", None, "seq"),
            P("dp", None, "seq"),
            P("dp", None, "seq"),
            P("dp", "seq", None),
            P("dp", "seq"),
            P("dp", None),
            P("dp", None),
        ),
        out_specs=(P("dp", None, "seq"), P("dp", None, "seq"), P("dp", None, "seq")),
        check_vma=False,
    )
```

```python
import functools

import jax
import jax.numpy as jnp
from jax import lax
from jax.experimental import pallas as pl
from jax.experimental.pallas import tpu as pltpu
from jax.sharding import PartitionSpec as P

HD = 128
RECUR = 4
GROUP = 128
CAP = 64
NX, NY, NZ = 4, 8, 8
SEQ = NX * GROUP
ROWS = NX * CAP
D = NY * NZ * 64
YB = D // NY
HALF = YB // 2
KC = D // 2
COLS = 512
HEADS = COLS // HD
VMEM = 48 * 1024 * 1024
NT = (((1,), (1,)), ((), ()))
TN = (((0,), (0,)), ((), ()))
bf16, f32 = jnp.bfloat16, jnp.float32
SENT = bf16


def _place(y, z, c):
    return ((y % NY) * NZ + z % NZ) * 2 + c


_ALL = [(y, z, c) for y in range(NY) for z in range(NZ) for c in range(2)]
Z_GROUPS = [[_place(y, z, c) for z in range(NZ)] for y in range(NY) for c in range(2)]
SWAP = [(_place(y, z, c), _place(y, z, 1 - c)) for y, z, c in _ALL]
Y_FIRST = [
    (_place(y, z, c), _place(y + 1 - 2 * (c ^ (z & 1)), z, c ^ (z & 1))) for y, z, c in _ALL
]
Y_ALONG = [(_place(y, z, c), _place(y + 1 - 2 * c, z, c)) for y, z, c in _ALL]
Z_SWAP = [(_place(y, z, c), _place(y, z ^ 1, c)) for y, z, c in _ALL]
X_ALONG, X_AGAINST = (
    [
        (_place(y, z, c) * NX + x, _place(y, z, c) * NX + (x + way * (1 - 2 * c)) % NX)
        for y, z, c in _ALL
        for x in range(NX)
    ]
    for way in (1, -1)
)


def _dot(a, b, dims=(((1,), (0,)), ((), ()))):
    return lax.dot_general(a, b, dims, preferred_element_type=f32)


def _selection(depth_row):
    live = (depth_row >= RECUR).astype(f32)
    live8 = jnp.broadcast_to(live, (8, GROUP)).astype(bf16)
    before = (
        lax.broadcasted_iota(jnp.int32, (GROUP, GROUP), 0)
        < lax.broadcasted_iota(jnp.int32, (GROUP, GROUP), 1)
    ).astype(bf16)
    rank = _dot(live8, before)[0:1].astype(jnp.int32)
    rank = jnp.where(live > 0.0, rank, -1)
    slot = lax.broadcasted_iota(jnp.int32, (CAP, GROUP), 0)
    return (slot == rank).astype(bf16)


def _cotangent_kernel(depths_any, grad_any, keep_ref, send_ref, q_ref, o_ref, depths_ref, grad_ref, sems):
    loads = [
        pltpu.make_async_copy(depths_any, depths_ref, sems.at[0]),
        pltpu.make_async_copy(grad_any, grad_ref, sems.at[1]),
    ]
    for load in loads:
        load.start()
    dp = lax.axis_index("dp")
    x = lax.axis_index("seq")
    core = lax.rem(dp, 2)
    odd = lax.rem(lax.div(dp, 2), 2)
    y = lax.div(dp, 2 * NZ)
    step = 1 - 2 * core
    l = lax.broadcasted_iota(jnp.int32, (256, 256), 0)
    m = lax.broadcasted_iota(jnp.int32, (256, 256), 1)
    other = jnp.bitwise_xor(jnp.bitwise_and(l >> 5, 1), jnp.bitwise_xor(core, odd))
    sort = (m == other * 128 + (l >> 6) * 32 + jnp.bitwise_and(l, 31)).astype(bf16)
    loads[0].wait()
    sel = _selection(depths_ref[:, pl.ds(pl.multiple_of(x * GROUP, GROUP), GROUP)])
    loads[1].wait()
    rows = _dot(sel, grad_ref[0]).astype(bf16)
    for n in range(D // 256):
        at = slice(n * 128, (n + 1) * 128)
        pair = _dot(rows[:, n * 256 : (n + 1) * 256], sort).astype(bf16)
        q_ref[:, at] = pair[:, :128]
        o_ref[:, at] = pair[:, 128:]

    def block(ref, index):
        index = lax.rem(index + 4 * NY, NY)
        return ref[:, pl.ds(pl.multiple_of(index * HALF, HALF), HALF)]

    def put(ref, j, value):
        ref[:, j * HALF : (j + 1) * HALF] = value

    own_q, own_o = block(q_ref, y), block(o_ref, y)
    put(keep_ref, 0, jnp.where(odd == 0, own_q, own_o))
    put(send_ref, 0, jnp.where(odd == 0, own_o, own_q))
    put(keep_ref, 7, block(q_ref, y + NY // 2))
    put(send_ref, 7, block(o_ref, y + NY // 2))
    for h in range(1, NY // 2):
        put(keep_ref, 2 * h - 1, block(q_ref, y - h * step))
        put(keep_ref, 2 * h, block(o_ref, y - h * step))
        put(send_ref, 2 * h - 1, block(o_ref, y + h * step))
        put(send_ref, 2 * h, block(q_ref, y + h * step))


def _softmax_kernel(
    depths_ref, documents_ref, q_ref, k_ref, v_ref, qc_ref, kc_ref, vc_ref, probs_ref, turned_ref, attended_ref, place_ref
):
    docs_col, docs_row, valid_col, valid_row = [], [], [], []
    for b in range(NX):
        at = slice(b * GROUP, (b + 1) * GROUP)
        to = slice(b * CAP, (b + 1) * CAP)
        sel = _selection(depths_ref[:, at])
        place_ref[at, :] = sel.astype(f32).T.astype(bf16)
        for src, dst in ((q_ref, qc_ref), (k_ref, kc_ref), (v_ref, vc_ref)):
            dst[to, :] = _dot(sel, src[0, at, :]).astype(bf16)
        docs = documents_ref[:, at].astype(f32)
        docs8 = jnp.broadcast_to(docs, (8, GROUP)).astype(bf16)
        ones8 = jnp.ones((8, GROUP), bf16)
        picked = sel.astype(f32)
        docs_col.append(jnp.sum(picked * docs, axis=1, keepdims=True))
        valid_col.append(jnp.sum(picked, axis=1, keepdims=True))
        docs_row.append(_dot(docs8, sel, NT)[0:1])
        valid_row.append(_dot(ones8, sel, NT)[0:1])
    doc_c = jnp.concatenate(docs_col, axis=0)
    doc_r = jnp.concatenate(docs_row, axis=1)
    val_c = jnp.concatenate(valid_col, axis=0)
    val_r = jnp.concatenate(valid_row, axis=1)
    doc_c = jnp.where(val_c > 0.5, doc_c, -1.0)
    doc_r = jnp.where(val_r > 0.5, doc_r, -2.0)
    i = lax.broadcasted_iota(jnp.int32, (ROWS, ROWS), 0)
    j = lax.broadcasted_iota(jnp.int32, (ROWS, ROWS), 1)
    allowed = (doc_c == doc_r) & (j <= i)
    scale = HD ** (-0.5)
    for h in range(HEADS):
        cols = slice(h * HD, (h + 1) * HD)
        scores = _dot(qc_ref[:, cols], kc_ref[:, cols], NT) * scale
        masked = jnp.where(allowed, scores, -1e30)
        top = jnp.max(masked, axis=1, keepdims=True)
        raw = jnp.where(allowed, jnp.exp(masked - top), 0.0)
        total = jnp.sum(raw, axis=1, keepdims=True)
        total = jnp.where(total > 0.0, total, 1.0)
        probs = raw * (1.0 / total)
        probs_ref[h] = probs
        turned_ref[h] = probs.T.astype(bf16)
        attended_ref[:, cols] = _dot(probs.astype(bf16), vc_ref[:, cols])


def _partial(g_refs, w_refs, start):
    total = None
    for n, w_ref in enumerate(w_refs):
        cols = slice(start + n * HALF, start + (n + 1) * HALF)
        term = _dot(jnp.concatenate([g[:, cols] for g in g_refs], axis=0), w_ref[...])
        total = term if total is None else total + term
    return total


def _project_first_kernel(own_ref, a1_ref, b1_ref, a2_ref, b2_ref, g0_ref, g1_ref, g2_ref, g3_ref, out_ref):
    out_ref[...] = _partial(
        (g0_ref, g1_ref, g2_ref, g3_ref), (own_ref, a1_ref, b1_ref, a2_ref, b2_ref), 0
    )


def _project_last_kernel(own, first_ref, a3_ref, b3_ref, a4_ref, g0_ref, g1_ref, g2_ref, g3_ref, out_ref):
    x = lax.axis_index("seq")
    step = 1 - 2 * lax.rem(lax.axis_index("dp"), 2)
    part = slice(0, CAP) if own else slice(CAP, 2 * CAP)
    gs = [g.at[part] for g in (g0_ref, g1_ref, g2_ref, g3_ref)]
    total = _partial(gs, (a3_ref, b3_ref, a4_ref), 5 * HALF)
    for n, shift in enumerate((0, -step, 2, step)):
        at = pl.ds(pl.multiple_of(lax.rem(x + shift + NX, NX) * CAP, CAP), CAP)
        frm = slice(2 * n * CAP + part.start, 2 * n * CAP + part.stop)
        out_ref[at, :] = (total[n * CAP : (n + 1) * CAP] + first_ref[frm, :]).astype(out_ref.dtype)


def _gradients_kernel(
    mine_ref, other_ref, qc_ref, kc_ref, vc_ref, probs_ref, turned_ref, attended_ref, place_ref,
    dq_any, dk_any, dv_any, og_ref, rows_ref, dq_ref, dk_ref, dv_ref, sems,
):
    scale = HD ** (-0.5)
    og_ref[...] = (mine_ref[...] + other_ref[...].astype(f32)).astype(bf16)
    heads = [slice(h * HD, (h + 1) * HD) for h in range(HEADS)]

    def finish(n, full_ref, out_any):
        for b in range(NX):
            at = slice(b * GROUP, (b + 1) * GROUP)
            full_ref[0, at, :] = _dot(place_ref[at, :], rows_ref[n, b * CAP : (b + 1) * CAP, :]).astype(bf16)
        copy = pltpu.make_async_copy(full_ref, out_any, sems.at[n])
        copy.start()
        return copy

    for h, cols in enumerate(heads):
        rows_ref[2, :, cols] = _dot(turned_ref[h], og_ref[:, cols]).astype(bf16)
    copies = [finish(2, dv_ref, dv_any)]
    dscores = []
    for h, cols in enumerate(heads):
        out_grad = og_ref[:, cols]
        delta = jnp.sum(out_grad.astype(f32) * attended_ref[:, cols], axis=1, keepdims=True)
        dscore = (probs_ref[h] * (_dot(out_grad, vc_ref[:, cols], NT) - delta)).astype(bf16)
        rows_ref[0, :, cols] = (_dot(dscore, kc_ref[:, cols]) * scale).astype(bf16)
        dscores.append(dscore)
    copies.append(finish(0, dq_ref, dq_any))
    for h, cols in enumerate(heads):
        rows_ref[1, :, cols] = (_dot(dscores[h], qc_ref[:, cols], TN) * scale).astype(bf16)
    copies.append(finish(1, dk_ref, dk_any))
    for copy in copies:
        copy.wait()


def _call(kernel, outs, flops, nbytes, exps=0, scratch=(), **specs):
    return pl.pallas_call(
        kernel,
        out_shape=tuple(jax.ShapeDtypeStruct(s, t) for s, t in outs),
        scratch_shapes=scratch,
        **specs,
        compiler_params=pltpu.CompilerParams(vmem_limit_bytes=VMEM),
        cost_estimate=pl.CostEstimate(flops=flops, bytes_accessed=nbytes, transcendentals=exps),
    )


def on_device(queries, key_states, value_states, grad_out, out_weight, depths, documents):
    keep, send = _call(
        _cotangent_kernel,
        [((CAP, KC), bf16)] * 2,
        2 * CAP * D * (GROUP + 256),
        2 << 20,
        scratch=[pltpu.VMEM((CAP, KC), bf16)] * 2
        + [
            pltpu.VMEM((1, SEQ), jnp.int32),
            pltpu.VMEM((1, GROUP, D), bf16),
            pltpu.SemaphoreType.DMA((2,)),
        ],
        in_specs=[pl.BlockSpec(memory_space=pl.ANY)] * 2,
    )(depths, grad_out)
    got = [lax.ppermute(send[n * CAP // 2 : (n + 1) * CAP // 2], "dp", SWAP) for n in range(2)]
    g0 = jnp.concatenate([keep, *got], axis=0)
    copies = jnp.broadcast_to(out_weight[None], (NZ,) + out_weight.shape)
    own = lax.all_to_all(copies, "dp", 0, 0, axis_index_groups=Z_GROUPS).reshape(HALF, COLS)
    g1 = lax.ppermute(g0, ("dp", "seq"), X_ALONG)
    g3 = lax.ppermute(g0, ("dp", "seq"), X_AGAINST)
    g2 = lax.ppermute(g1, ("dp", "seq"), X_ALONG)
    a1 = lax.ppermute(own, "dp", Y_FIRST)
    a1, g1 = lax.optimization_barrier((a1, g1))
    a2 = lax.ppermute(a1, "dp", Y_ALONG)
    b1 = lax.ppermute(a1, "dp", Z_SWAP)
    a2, g3 = lax.optimization_barrier((a2, g3))
    a3 = lax.ppermute(a2, "dp", Y_ALONG)
    b2 = lax.ppermute(a2, "dp", Z_SWAP)
    a3, b1, g2 = lax.optimization_barrier((a3, b1, g2))
    a4 = lax.ppermute(a3, "dp", Y_ALONG)
    b3 = lax.ppermute(a3, "dp", Z_SWAP)
    qc, kc, vc, probs, turned, attended, place = _call(
        _softmax_kernel,
        [((ROWS, COLS), bf16)] * 3
        + [((HEADS, ROWS, ROWS), f32), ((HEADS, ROWS, ROWS), bf16), ((ROWS, COLS), f32), ((SEQ, CAP), bf16)],
        4 * HEADS * ROWS * ROWS * HD,
        4 << 20,
        HEADS * ROWS * ROWS,
    )(depths, documents, queries, key_states, value_states)
    first = _call(
        _project_first_kernel, [((2 * ROWS, COLS), f32)], 20 * ROWS * HALF * COLS, 5 << 20
    )(own, a1, b1, a2, b2, g0, g1, g2, g3)[0]
    first, probs = lax.optimization_barrier((first, probs))
    last = (first, a3, b3, a4, g0, g1, g2, g3)
    other = _call(
        functools.partial(_project_last_kernel, False), [((ROWS, COLS), SENT)], 6 * ROWS * HALF * COLS, 3 << 20
    )(*last)[0]
    swapped = lax.ppermute(other, "dp", SWAP)
    mine = _call(
        functools.partial(_project_last_kernel, True), [((ROWS, COLS), f32)], 6 * ROWS * HALF * COLS, 3 << 20
    )(*last)[0]
    return _call(
        _gradients_kernel,
        [((1, SEQ, COLS), bf16)] * 3,
        10 * HEADS * ROWS * ROWS * HD,
        5 << 20,
        scratch=[pltpu.VMEM((ROWS, COLS), bf16), pltpu.VMEM((3, ROWS, COLS), bf16)]
        + [pltpu.VMEM((1, SEQ, COLS), bf16)] * 3
        + [pltpu.SemaphoreType.DMA((3,))],
        out_specs=tuple([pl.BlockSpec(memory_space=pl.ANY)] * 3),
    )(mine, swapped, qc, kc, vc, probs, turned, attended, place)


def solution(mesh):
    return jax.shard_map(
        on_device,
        mesh=mesh,
        in_specs=(
            P("dp", None, "seq"),
            P("dp", None, "seq"),
            P("dp", None, "seq"),
            P("dp", "seq", None),
            P("dp", "seq"),
            P("dp", None),
            P("dp", None),
        ),
        out_specs=(P("dp", None, "seq"), P("dp", None, "seq"), P("dp", None, "seq")),
        check_vma=False,
    )
```

```python
import functools

import jax
import jax.numpy as jnp
from jax import lax
from jax.experimental import pallas as pl
from jax.experimental.pallas import tpu as pltpu
from jax.sharding import PartitionSpec as P

HD = 128
RECUR = 4
GROUP = 128
CAP = 64
NX, NY, NZ = 4, 8, 8
SEQ = NX * GROUP
ROWS = NX * CAP
D = NY * NZ * 64
YB = D // NY
HALF = YB // 2
KC = D // 2
COLS = 512
HEADS = COLS // HD
VMEM = 48 * 1024 * 1024
NT = (((1,), (1,)), ((), ()))
TN = (((0,), (0,)), ((), ()))
bf16, f32 = jnp.bfloat16, jnp.float32
SENT = bf16


def _place(y, z, c):
    return ((y % NY) * NZ + z % NZ) * 2 + c


_ALL = [(y, z, c) for y in range(NY) for z in range(NZ) for c in range(2)]
Z_GROUPS = [[_place(y, z, c) for z in range(NZ)] for y in range(NY) for c in range(2)]
SWAP = [(_place(y, z, c), _place(y, z, 1 - c)) for y, z, c in _ALL]
Y_FIRST = [
    (_place(y, z, c), _place(y + 1 - 2 * (c ^ (z & 1)), z, c ^ (z & 1))) for y, z, c in _ALL
]
Y_ALONG = [(_place(y, z, c), _place(y + 1 - 2 * c, z, c)) for y, z, c in _ALL]
Z_SWAP = [(_place(y, z, c), _place(y, z ^ 1, c)) for y, z, c in _ALL]
X_ALONG, X_AGAINST = (
    [
        (_place(y, z, c) * NX + x, _place(y, z, c) * NX + (x + way * (1 - 2 * c)) % NX)
        for y, z, c in _ALL
        for x in range(NX)
    ]
    for way in (1, -1)
)


def _dot(a, b, dims=(((1,), (0,)), ((), ()))):
    return lax.dot_general(a, b, dims, preferred_element_type=f32)


def _selection(depth_row):
    live = (depth_row >= RECUR).astype(f32)
    live8 = jnp.broadcast_to(live, (8, GROUP)).astype(bf16)
    before = (
        lax.broadcasted_iota(jnp.int32, (GROUP, GROUP), 0)
        < lax.broadcasted_iota(jnp.int32, (GROUP, GROUP), 1)
    ).astype(bf16)
    rank = _dot(live8, before)[0:1].astype(jnp.int32)
    rank = jnp.where(live > 0.0, rank, -1)
    slot = lax.broadcasted_iota(jnp.int32, (CAP, GROUP), 0)
    return (slot == rank).astype(bf16)


def _cotangent_kernel(depths_any, grad_any, keep_ref, send_ref, q_ref, o_ref, depths_ref, grad_ref, sems):
    loads = [
        pltpu.make_async_copy(depths_any, depths_ref, sems.at[0]),
        pltpu.make_async_copy(grad_any, grad_ref, sems.at[1]),
    ]
    for load in loads:
        load.start()
    dp = lax.axis_index("dp")
    x = lax.axis_index("seq")
    core = lax.rem(dp, 2)
    odd = lax.rem(lax.div(dp, 2), 2)
    y = lax.div(dp, 2 * NZ)
    step = 1 - 2 * core
    l = lax.broadcasted_iota(jnp.int32, (256, 256), 0)
    m = lax.broadcasted_iota(jnp.int32, (256, 256), 1)
    other = jnp.bitwise_xor(jnp.bitwise_and(l >> 5, 1), jnp.bitwise_xor(core, odd))
    sort = (m == other * 128 + (l >> 6) * 32 + jnp.bitwise_and(l, 31)).astype(bf16)
    loads[0].wait()
    sel = _selection(depths_ref[:, pl.ds(pl.multiple_of(x * GROUP, GROUP), GROUP)])
    loads[1].wait()
    rows = _dot(sel, grad_ref[0]).astype(bf16)
    for n in range(D // 256):
        at = slice(n * 128, (n + 1) * 128)
        pair = _dot(rows[:, n * 256 : (n + 1) * 256], sort).astype(bf16)
        q_ref[:, at] = pair[:, :128]
        o_ref[:, at] = pair[:, 128:]

    def block(ref, index):
        index = lax.rem(index + 4 * NY, NY)
        return ref[:, pl.ds(pl.multiple_of(index * HALF, HALF), HALF)]

    def put(ref, j, value):
        ref[:, j * HALF : (j + 1) * HALF] = value

    own_q, own_o = block(q_ref, y), block(o_ref, y)
    put(keep_ref, 0, jnp.where(odd == 0, own_q, own_o))
    put(send_ref, 0, jnp.where(odd == 0, own_o, own_q))
    put(keep_ref, 7, block(q_ref, y + NY // 2))
    put(send_ref, 7, block(o_ref, y + NY // 2))
    for h in range(1, NY // 2):
        put(keep_ref, 2 * h - 1, block(q_ref, y - h * step))
        put(keep_ref, 2 * h, block(o_ref, y - h * step))
        put(send_ref, 2 * h - 1, block(o_ref, y + h * step))
        put(send_ref, 2 * h, block(q_ref, y + h * step))


def _softmax_kernel(
    depths_ref, documents_ref, q_ref, k_ref, v_ref, qc_ref, kc_ref, vc_ref, probs_ref, turned_ref, attended_ref, place_ref
):
    docs_col, docs_row, valid_col, valid_row = [], [], [], []
    for b in range(NX):
        at = slice(b * GROUP, (b + 1) * GROUP)
        to = slice(b * CAP, (b + 1) * CAP)
        sel = _selection(depths_ref[:, at])
        place_ref[at, :] = sel.astype(f32).T.astype(bf16)
        for src, dst in ((q_ref, qc_ref), (k_ref, kc_ref), (v_ref, vc_ref)):
            dst[to, :] = _dot(sel, src[0, at, :]).astype(bf16)
        docs = documents_ref[:, at].astype(f32)
        docs8 = jnp.broadcast_to(docs, (8, GROUP)).astype(bf16)
        ones8 = jnp.ones((8, GROUP), bf16)
        picked = sel.astype(f32)
        docs_col.append(jnp.sum(picked * docs, axis=1, keepdims=True))
        valid_col.append(jnp.sum(picked, axis=1, keepdims=True))
        docs_row.append(_dot(docs8, sel, NT)[0:1])
        valid_row.append(_dot(ones8, sel, NT)[0:1])
    doc_c = jnp.concatenate(docs_col, axis=0)
    doc_r = jnp.concatenate(docs_row, axis=1)
    val_c = jnp.concatenate(valid_col, axis=0)
    val_r = jnp.concatenate(valid_row, axis=1)
    doc_c = jnp.where(val_c > 0.5, doc_c, -1.0)
    doc_r = jnp.where(val_r > 0.5, doc_r, -2.0)
    i = lax.broadcasted_iota(jnp.int32, (ROWS, ROWS), 0)
    j = lax.broadcasted_iota(jnp.int32, (ROWS, ROWS), 1)
    allowed = (doc_c == doc_r) & (j <= i)
    scale = HD ** (-0.5)
    for h in range(HEADS):
        cols = slice(h * HD, (h + 1) * HD)
        scores = _dot(qc_ref[:, cols], kc_ref[:, cols], NT) * scale
        masked = jnp.where(allowed, scores, -1e30)
        top = jnp.max(masked, axis=1, keepdims=True)
        raw = jnp.where(allowed, jnp.exp(masked - top), 0.0)
        total = jnp.sum(raw, axis=1, keepdims=True)
        total = jnp.where(total > 0.0, total, 1.0)
        probs = raw * (1.0 / total)
        probs_ref[h] = probs
        turned_ref[h] = probs.T.astype(bf16)
        attended_ref[:, cols] = _dot(probs.astype(bf16), vc_ref[:, cols])


def _partial(g_refs, w_refs, start):
    total = None
    for n, w_ref in enumerate(w_refs):
        cols = slice(start + n * HALF, start + (n + 1) * HALF)
        term = _dot(jnp.concatenate([g[:, cols] for g in g_refs], axis=0), w_ref[...])
        total = term if total is None else total + term
    return total


def _project_first_kernel(own_ref, a1_ref, b1_ref, a2_ref, b2_ref, g0_ref, g1_ref, g2_ref, g3_ref, out_ref):
    out_ref[...] = _partial(
        (g0_ref, g1_ref, g2_ref, g3_ref), (own_ref, a1_ref, b1_ref, a2_ref, b2_ref), 0
    )


def _project_last_kernel(own, first_ref, a3_ref, b3_ref, a4_ref, g0_ref, g1_ref, g2_ref, g3_ref, out_ref):
    x = lax.axis_index("seq")
    step = 1 - 2 * lax.rem(lax.axis_index("dp"), 2)
    part = slice(0, CAP) if own else slice(CAP, 2 * CAP)
    gs = [g.at[part] for g in (g0_ref, g1_ref, g2_ref, g3_ref)]
    total = _partial(gs, (a3_ref, b3_ref, a4_ref), 5 * HALF)
    for n, shift in enumerate((0, -step, 2, step)):
        at = pl.ds(pl.multiple_of(lax.rem(x + shift + NX, NX) * CAP, CAP), CAP)
        frm = slice(2 * n * CAP + part.start, 2 * n * CAP + part.stop)
        out_ref[at, :] = (total[n * CAP : (n + 1) * CAP] + first_ref[frm, :]).astype(out_ref.dtype)


def _gradients_kernel(
    mine_ref, other_ref, qc_ref, kc_ref, vc_ref, probs_ref, turned_ref, attended_ref, place_ref,
    dq_any, dk_any, dv_any, og_ref, rows_ref, dq_ref, dk_ref, dv_ref, sems,
):
    scale = HD ** (-0.5)
    og_ref[...] = (mine_ref[...] + other_ref[...].astype(f32)).astype(bf16)
    heads = [slice(h * HD, (h + 1) * HD) for h in range(HEADS)]

    def finish(n, full_ref, out_any):
        for b in range(NX):
            at = slice(b * GROUP, (b + 1) * GROUP)
            full_ref[0, at, :] = _dot(place_ref[at, :], rows_ref[n, b * CAP : (b + 1) * CAP, :]).astype(bf16)
        copy = pltpu.make_async_copy(full_ref, out_any, sems.at[n])
        copy.start()
        return copy

    for h, cols in enumerate(heads):
        rows_ref[2, :, cols] = _dot(turned_ref[h], og_ref[:, cols]).astype(bf16)
    copies = [finish(2, dv_ref, dv_any)]
    dscores = []
    for h, cols in enumerate(heads):
        out_grad = og_ref[:, cols]
        delta = jnp.sum(out_grad.astype(f32) * attended_ref[:, cols], axis=1, keepdims=True)
        dscore = (probs_ref[h] * (_dot(out_grad, vc_ref[:, cols], NT) - delta)).astype(bf16)
        rows_ref[0, :, cols] = (_dot(dscore, kc_ref[:, cols]) * scale).astype(bf16)
        dscores.append(dscore)
    copies.append(finish(0, dq_ref, dq_any))
    for h, cols in enumerate(heads):
        rows_ref[1, :, cols] = (_dot(dscores[h], qc_ref[:, cols], TN) * scale).astype(bf16)
    copies.append(finish(1, dk_ref, dk_any))
    for copy in copies:
        copy.wait()


def _call(kernel, outs, flops, nbytes, exps=0, scratch=(), **specs):
    return pl.pallas_call(
        kernel,
        out_shape=tuple(jax.ShapeDtypeStruct(s, t) for s, t in outs),
        scratch_shapes=scratch,
        **specs,
        compiler_params=pltpu.CompilerParams(vmem_limit_bytes=VMEM),
        cost_estimate=pl.CostEstimate(flops=flops, bytes_accessed=nbytes, transcendentals=exps),
    )


def on_device(queries, key_states, value_states, grad_out, out_weight, depths, documents):
    keep, send = _call(
        _cotangent_kernel,
        [((CAP, KC), bf16)] * 2,
        2 * CAP * D * (GROUP + 256),
        2 << 20,
        scratch=[pltpu.VMEM((CAP, KC), bf16)] * 2
        + [
            pltpu.VMEM((1, SEQ), jnp.int32),
            pltpu.VMEM((1, GROUP, D), bf16),
            pltpu.SemaphoreType.DMA((2,)),
        ],
        in_specs=[pl.BlockSpec(memory_space=pl.ANY)] * 2,
    )(depths, grad_out)
    got = [lax.ppermute(send[n * CAP // 2 : (n + 1) * CAP // 2], "dp", SWAP) for n in range(2)]
    g0 = jnp.concatenate([keep, *got], axis=0)
    copies = jnp.stack([out_weight] * NZ)
    own = lax.all_to_all(copies, "dp", 0, 0, axis_index_groups=Z_GROUPS).reshape(HALF, COLS)
    g1 = lax.ppermute(g0, ("dp", "seq"), X_ALONG)
    g3 = lax.ppermute(g0, ("dp", "seq"), X_AGAINST)
    g2 = lax.ppermute(g1, ("dp", "seq"), X_ALONG)
    a1 = lax.ppermute(own, "dp", Y_FIRST)
    a1, g1 = lax.optimization_barrier((a1, g1))
    a2 = lax.ppermute(a1, "dp", Y_ALONG)
    b1 = lax.ppermute(a1, "dp", Z_SWAP)
    a2, g3 = lax.optimization_barrier((a2, g3))
    a3 = lax.ppermute(a2, "dp", Y_ALONG)
    b2 = lax.ppermute(a2, "dp", Z_SWAP)
    a3, b1 = lax.optimization_barrier((a3, b1))
    a4 = lax.ppermute(a3, "dp", Y_ALONG)
    b3 = lax.ppermute(a3, "dp", Z_SWAP)
    qc, kc, vc, probs, turned, attended, place = _call(
        _softmax_kernel,
        [((ROWS, COLS), bf16)] * 3
        + [((HEADS, ROWS, ROWS), f32), ((HEADS, ROWS, ROWS), bf16), ((ROWS, COLS), f32), ((SEQ, CAP), bf16)],
        4 * HEADS * ROWS * ROWS * HD,
        4 << 20,
        HEADS * ROWS * ROWS,
    )(depths, documents, queries, key_states, value_states)
    first = _call(
        _project_first_kernel, [((2 * ROWS, COLS), f32)], 20 * ROWS * HALF * COLS, 5 << 20
    )(own, a1, b1, a2, b2, g0, g1, g2, g3)[0]
    first, probs = lax.optimization_barrier((first, probs))
    last = (first, a3, b3, a4, g0, g1, g2, g3)
    other = _call(
        functools.partial(_project_last_kernel, False), [((ROWS, COLS), SENT)], 6 * ROWS * HALF * COLS, 3 << 20
    )(*last)[0]
    swapped = lax.ppermute(other, "dp", SWAP)
    mine = _call(
        functools.partial(_project_last_kernel, True), [((ROWS, COLS), f32)], 6 * ROWS * HALF * COLS, 3 << 20
    )(*last)[0]
    return _call(
        _gradients_kernel,
        [((1, SEQ, COLS), bf16)] * 3,
        10 * HEADS * ROWS * ROWS * HD,
        5 << 20,
        scratch=[pltpu.VMEM((ROWS, COLS), bf16), pltpu.VMEM((3, ROWS, COLS), bf16)]
        + [pltpu.VMEM((1, SEQ, COLS), bf16)] * 3
        + [pltpu.SemaphoreType.DMA((3,))],
        out_specs=tuple([pl.BlockSpec(memory_space=pl.ANY)] * 3),
    )(mine, swapped, qc, kc, vc, probs, turned, attended, place)


def solution(mesh):
    return jax.shard_map(
        on_device,
        mesh=mesh,
        in_specs=(
            P("dp", None, "seq"),
            P("dp", None, "seq"),
            P("dp", None, "seq"),
            P("dp", "seq", None),
            P("dp", "seq"),
            P("dp", None),
            P("dp", None),
        ),
        out_specs=(P("dp", None, "seq"), P("dp", None, "seq"), P("dp", None, "seq")),
        check_vma=False,
    )
```
